32 devices in a mesh: inp: 8 (over z, x), tm: 4 (over y, core).
Axes of the slice: x: 2, y: 2, z: 4, core: 2. Of those that a mesh axis runs over, the one named last changes fastest.
Arguments:
- voltages: float32 [256, 256, 2048], P('inp', 'tm'), may hold values from -6 to 6
- filter_taps: float32 [4, 2048], replicated, may hold values from -1 to 2
Outputs:
- visibilities: float32 [2, 1024, 256, 256], P(None, ('inp', 'tm'))
The draws below stay inside these ranges and needn't reach their ends.
All inputs are finite; a program needn't handle non-finite values.
Results may differ from the reference program's by a relative error of at most 0.000084.
Values sent between devices are 32-bit elements; how exact they have to be, the bound alone decides.
No kernel may reach another device: no remote copies, remote signals or barrier semaphores. Data moves between devices by JAX's collectives and lax.ppermute only.
A program may use at most 192 MiB of HBM per device.

```python
import math
import jax
import jax.numpy as jnp
from jax import lax

NI = 256
NFFT = 2048
TAPS = 4
CH = 1024
SPECTRA = 256


def draw_filter_taps(key, part):
    total = TAPS * NFFT
    position = jnp.arange(total, dtype=jnp.float32).reshape(TAPS, NFFT)
    centre = (total - 1) / 2.0
    window = 0.5 - 0.5 * jnp.cos(2.0 * math.pi * (position + 0.5) / total)
    proto = jnp.sinc((position - centre) / NFFT) * window
    rough = jax.random.uniform(key, (TAPS, NFFT), jnp.float32, 0.5, 1.5)
    return (proto * rough).astype(jnp.float32)


def block_levels(rng, extent, split, smallest, high):
    level = 1.0
    for dim, blocks in split:
        heights = jax.random.uniform(jax.random.fold_in(jax.random.fold_in(rng, 6), dim), (blocks,), jnp.float32, smallest / len(split), high / len(split))
        level = level * jnp.repeat(jnp.exp(heights), extent[dim] // blocks).reshape((-1,) + (1,) * (len(extent) - 1 - dim))
    return level


def normal_values(stream_key, shape, scale, reach, pieces=(), kind=jnp.bfloat16):
    values = jax.random.normal(stream_key, shape, jnp.float32) * scale
    if len(pieces) > 0:
        values = block_levels(stream_key, shape, pieces, -0.22, 0.18) * values
    return jnp.clip(values, min=-reach, max=reach).astype(kind)


def setup_inputs(seed: int = 0) -> dict:
    seeds = jax.random.split(jax.random.key(seed), 3)
    voltages = normal_values(seeds[0], (NI, SPECTRA, NFFT), 1.0, 6.0, ((0, 8), (1, 4)), jnp.float32)
    filter_taps = draw_filter_taps(jax.random.fold_in(seeds[2], 71), 0)
    return dict(voltages=voltages, filter_taps=filter_taps)


def reference(voltages, filter_taps):
    zeros = jnp.zeros((NI, TAPS - 1, NFFT), voltages.dtype)
    frames = jnp.concatenate([zeros, voltages], axis=1)
    filtered = filter_taps[0] * frames[:, 0:SPECTRA, :]
    for k in range(1, TAPS):
        filtered = filtered + filter_taps[k] * frames[:, k:k + SPECTRA, :]
    spec = jnp.fft.rfft(filtered, axis=-1)[:, :, :CH]
    spec_re = jnp.transpose(jnp.real(spec), (2, 0, 1)) / math.sqrt(NFFT)
    spec_im = jnp.transpose(jnp.imag(spec), (2, 0, 1)) / math.sqrt(NFFT)
    spec_re = spec_re.astype(voltages.dtype)
    spec_im = spec_im.astype(voltages.dtype)
    left = jnp.concatenate([spec_re, spec_im], axis=-1)
    twisted = jnp.concatenate([spec_im, -spec_re], axis=-1)
    block = 16
    left_b = left.reshape(CH // block, block, NI, 2 * SPECTRA)
    twisted_b = twisted.reshape(CH // block, block, NI, 2 * SPECTRA)

    def correlate(pair):
        plain, turned = pair
        real_part = jnp.einsum('cas,cbs->cab', plain, plain, precision=lax.Precision.HIGHEST)
        imag_part = jnp.einsum('cas,cbs->cab', turned, plain, precision=lax.Precision.HIGHEST)
        return jnp.stack([real_part, imag_part])
    result = lax.map(correlate, (left_b, twisted_b))
    result = jnp.transpose(result, (1, 0, 2, 3, 4)).reshape(2, CH, NI, NI)
    return result / SPECTRA
```

```python
import functools
import math

import jax
import jax.numpy as jnp
import ml_dtypes
import numpy as np
from jax import lax
from jax.experimental import pallas as pl
from jax.experimental.pallas import tpu as pltpu
from jax.sharding import PartitionSpec as P

AXES = ("inp", "tm")
GROUP = 8
BLOCK = 8
ROWS = GROUP * BLOCK
LANES = 128
PAIR = 16
VMEM_BYTES = 56 * 1024 * 1024
NT = (((1,), (1,)), ((), ()))


def fold_of(step, residue):
    if step % 4 == 0 and residue % 4 == 0:
        return "sum4"
    if step % 4 == 0 and residue % 4 == 2:
        return "alt4"
    if step % 2 == 0 and residue % 2 == 1:
        return "diff2"
    return "none"


def fold_terms(nfft, fold):
    return {"sum4": nfft // 4, "alt4": nfft // 4, "diff2": nfft // 2, "none": nfft}[fold]


def transform_table(nfft, ch_dev, count, step, residue):
    depth = fold_terms(nfft, fold_of(step, residue))
    dest = np.arange(count)[:, None]
    channel = dest * ch_dev + step * np.arange(GROUP)[None, :] + residue
    phase = channel[:, :, None] * np.arange(depth)[None, None, :] % nfft
    angle = 2.0 * math.pi / nfft * phase.astype(np.float64)
    scale = 1.0 / math.sqrt(nfft)
    table = np.concatenate([np.cos(angle), -np.sin(angle)], axis=1) * scale
    high = table.astype(ml_dtypes.bfloat16)
    low = (table - high.astype(np.float64)).astype(ml_dtypes.bfloat16)
    return high, low


def split(value):
    high = value.astype(jnp.bfloat16)
    return high, (value - high.astype(jnp.float32)).astype(jnp.bfloat16)


def dot_nt(a, b):
    return lax.dot_general(a, b, dimension_numbers=NT, preferred_element_type=jnp.float32)


def swap_halves(lane, a, b, width):
    first = lane % (2 * width) < width
    return (
        jnp.where(first, a, pltpu.roll(b, width, 1)),
        jnp.where(first, pltpu.roll(a, LANES - width, 1), b),
    )


def transform_kernel(folds, tiles, has_base, has_tail, taps_ref, *rest):
    x_refs, rest = rest[:tiles], rest[tiles:]
    before_refs, rest = rest[:tiles], rest[tiles:]
    tables, rest = rest[: 2 * len(folds)], rest[2 * len(folds) + has_base :]
    out, rest = rest[0], rest[1:]
    if has_tail:
        tail, rest = rest[0], rest[1:]
    folded, head = rest[: 2 * len(folds)], rest[2 * len(folds)]
    block, frames, _ = x_refs[0].shape
    count = out.shape[0]
    taps = taps_ref.shape[0]
    past = taps - 1
    quarter = tiles // 4

    if has_tail:

        for i in range(block):
            for tile in range(tiles):
                for r in range(past):
                    row = x_refs[tile][i, frames - past + r : frames - past + r + 1, :]
                    tail[i * past + r : i * past + r + 1, tile * LANES : (tile + 1) * LANES] = row

    def weights(tile):
        columns = slice(tile * LANES, (tile + 1) * LANES)
        return [taps_ref[k : k + 1, columns] for k in range(taps)]

    def fill_head(slot, i, tile):
        if has_tail:
            head[slot, 0:8, :] = before_refs[tile][i]
        else:
            for r in range(past):
                head[slot, 8 - past + r : 9 - past + r, :] = before_refs[tile][pl.ds(i * past + r, 1), :]
        head[slot, 8 : 8 + PAIR, :] = x_refs[tile][i, 0:PAIR, :]

    def window(slot, i, tile, start):
        if start < taps:
            return head[slot, pl.ds(8 + start, 8, stride=2), :]
        return x_refs[tile][i, pl.ds(start, 8, stride=2), :]

    def filtered(slot, i, tile, first, tap_rows):
        loads = [window(slot, i, tile, first + 1 - back) for back in range(taps + 1)]
        halves = []
        for odd in (0, 1):
            total = tap_rows[taps - 1] * loads[1 - odd]
            for back in range(1, taps):
                total = total + tap_rows[taps - 1 - back] * loads[1 - odd + back]
            halves.append(total)
        return jnp.concatenate(halves, axis=0)

    def store(which, rows, tile, value):
        high, low = split(value)
        columns = slice(tile * LANES, (tile + 1) * LANES)
        folded[2 * which][rows, columns] = high
        folded[2 * which + 1][rows, columns] = low

    for tile in range(tiles if "none" in folds else quarter):
        sources = [tile] if "none" in folds else [tile + q * quarter for q in range(4)]

        @pl.loop(0, block)
        def _(i):
            tap_rows = [weights(source) for source in sources]
            for slot, source in enumerate(sources):
                fill_head(slot, i, source)
            for first in range(0, frames, PAIR):
                rows = pl.ds(pl.multiple_of(i * frames + first, PAIR), PAIR)
                f = [
                    filtered(slot, i, source, first, tap_rows[slot])
                    for slot, source in enumerate(sources)
                ]
                for which, fold in enumerate(folds):
                    if fold == "none":
                        store(which, rows, tile, f[0])
                    elif fold == "sum4":
                        store(which, rows, tile, (f[0] + f[2]) + (f[1] + f[3]))
                    elif fold == "alt4":
                        store(which, rows, tile, (f[0] + f[2]) - (f[1] + f[3]))
                    else:
                        store(which, rows, tile, f[0] - f[2])
                        store(which, rows, tile + quarter, f[1] - f[3])

    lane = lax.broadcasted_iota(jnp.int32, (GROUP, LANES), 1)
    together = min(16, count)
    for start in range(0, count, together):
        rows = slice(start * 2 * GROUP, (start + together) * 2 * GROUP)
        specs = []
        for which in range(len(folds)):
            a_hi, a_lo = tables[2 * which][rows], tables[2 * which + 1][rows]
            g_hi, g_lo = folded[2 * which], folded[2 * which + 1]
            specs.append(dot_nt(a_hi, g_hi[...]) + dot_nt(a_lo, g_hi[...]) + dot_nt(a_hi, g_lo[...]))
        for k in range(together):
            top = 2 * GROUP * k
            parts = [s[top + h * GROUP : top + (h + 1) * GROUP] for s in specs for h in (0, 1)]
            for at in range(0, block * frames // LANES):
                tiles_at = [p[:, at * LANES : (at + 1) * LANES] for p in parts]
                if len(parts) == 2:
                    mixed = swap_halves(lane, tiles_at[0], tiles_at[1], LANES // 2)
                else:
                    u0, u2 = swap_halves(lane, tiles_at[0], tiles_at[2], LANES // 2)
                    u1, u3 = swap_halves(lane, tiles_at[1], tiles_at[3], LANES // 2)
                    mixed = swap_halves(lane, u0, u1, LANES // 4) + swap_halves(lane, u2, u3, LANES // 4)
                for j, tile in enumerate(mixed):
                    i = at * len(parts) + j
                    out[start + k, pl.ds(i, GROUP, stride=block), :] = tile


def transform(voltages, before, filter_taps, count, ch_dev, step, residues, half, span, size, at, base=None):
    inputs_dev, frames, nfft = voltages.shape
    past = filter_taps.shape[0] - 1
    folds = [fold_of(step, residue) for residue in residues]
    tiles = nfft // LANES
    if half is not None:
        frames = frames // 2
    low, high = span
    blocks = high - low
    has_base = int(base is not None)
    has_tail = half == 1
    operands = []
    specs = []

    def add(operand, spec):
        operands.append(operand)
        specs.append(spec)

    add(filter_taps, pl.BlockSpec(filter_taps.shape, lambda b: (0, 0)))
    for tile in range(tiles):
        add(voltages, pl.BlockSpec((BLOCK, frames, LANES), lambda b, t=tile: (b + low, half or 0, t)))
    for tile in range(tiles):
        if has_tail:
            add(
                voltages,
                pl.BlockSpec((BLOCK, 8, LANES), lambda b, t=tile: (b + low, frames // 8 - 1, t)),
            )
        else:
            add(before, pl.BlockSpec((BLOCK * past, LANES), lambda b, t=tile: (b + low, t)))
    scratch = []
    flops = 0
    for residue, fold in zip(residues, folds):
        depth = fold_terms(nfft, fold)
        for table in transform_table(nfft, ch_dev, count, step, residue):
            table = table.reshape(-1, depth)
            add(
                jnp.asarray(table),
                pl.BlockSpec(table.shape, lambda b: (0, 0), pipeline_mode=pl.Buffered(1)),
            )
        scratch += [pltpu.VMEM((BLOCK * frames, depth), jnp.bfloat16)] * 2
        flops += 6 * 2 * GROUP * count * depth * blocks * BLOCK * frames
    scratch.append(pltpu.VMEM((4, 8 + PAIR, LANES), jnp.float32))
    aliases = {}
    if has_base:
        aliases[len(operands)] = 0
        add(base, pl.BlockSpec(memory_space=pl.ANY))
    shapes = [jax.ShapeDtypeStruct((count, size * ROWS, LANES), jnp.float32)]
    out_specs = [pl.BlockSpec((count, ROWS, LANES), lambda b: (0, b + at, 0))]
    if has_tail:
        shapes.append(jax.ShapeDtypeStruct((blocks * BLOCK * past, nfft), jnp.float32))
        out_specs.append(pl.BlockSpec((BLOCK * past, nfft), lambda b: (b, 0)))
    return pl.pallas_call(
        functools.partial(transform_kernel, folds, tiles, has_base, has_tail),
        grid=(blocks,),
        out_shape=shapes,
        input_output_aliases=aliases,
        in_specs=specs,
        out_specs=out_specs,
        scratch_shapes=scratch,
        compiler_params=pltpu.CompilerParams(vmem_limit_bytes=VMEM_BYTES),
        cost_estimate=pl.CostEstimate(
            flops=flops, bytes_accessed=4 * blocks * BLOCK * frames * nfft, transcendentals=0
        ),
        name="spectra_" + "_".join(map(str, residues)) + ("" if half is None else f"_half{half}"),
    )(*operands)


def correlate_kernel(n_inp, n_tm, frames, pieces, together, has_base, *rest):
    streams = []
    for number in pieces:
        streams.append(rest[:number])
        rest = rest[number:]
    (out,) = rest[has_base:]
    scale = 1.0 / (n_tm * frames)
    width = LANES // 2 // len(pieces)
    first = lax.broadcasted_iota(jnp.int32, (1, LANES), 1) % (2 * width) < width
    low_half = lax.broadcasted_iota(jnp.int32, (1, LANES), 1) < LANES // 2

    def payload(stream, sender, c):
        rows = slice(c * BLOCK, (c + 1) * BLOCK)
        return [
            array[sender, b, rows, :] for array in streams[stream] for b in range(array.shape[1])
        ]

    for c in range(together):
        columns = []
        for t in range(n_tm):
            senders = [p * n_tm + t for p in range(n_inp)]
            value = jnp.concatenate([x for s in senders for x in payload(0, s, c)], axis=0)
            if len(pieces) == 1:
                turned = pltpu.roll(value, width, 1)
                turned = jnp.where(first, turned, -turned)
            else:
                other = jnp.concatenate([x for s in senders for x in payload(1, s, c)], axis=0)
                turn = pl.program_id(1) * (LANES // 2)
                value = jnp.where(
                    low_half, pltpu.roll(value, turn, 1), pltpu.roll(other, LANES // 2 - turn, 1)
                )
                turned = jnp.where(
                    first, pltpu.roll(value, LANES - width, 1), -pltpu.roll(value, width, 1)
                )
            columns.append(split(value) + split(turned))
        p_hi, p_lo, t_hi, t_lo = [jnp.concatenate(column, axis=1) for column in zip(*columns)]
        right = jnp.concatenate([p_hi, p_hi, p_lo], axis=1)
        out[0, c, 0] = dot_nt(jnp.concatenate([p_hi, p_lo, p_hi], axis=1), right) * scale
        out[1, c, 0] = dot_nt(jnp.concatenate([t_hi, t_lo, t_hi], axis=1), right) * scale


def correlate(streams, base, n_inp, n_tm, inputs_dev, frames, ch_dev, step, residues):
    count = n_inp * n_tm
    n_inputs = n_inp * inputs_dev
    has_base = int(base is not None)
    together = 2
    operands = []
    specs = []
    for stream in streams:
        for array, number, at in stream:
            operands.append(array.reshape(count, -1, ROWS, LANES))
            specs.append(
                pl.BlockSpec(
                    (count, number, together * BLOCK, LANES),
                    lambda c, r, q=at // number: (0, q, c, 0),
                )
            )
    aliases = {}
    if has_base:
        aliases[len(operands)] = 0
        operands.append(base)
        specs.append(pl.BlockSpec(memory_space=pl.ANY))
    gap = residues[-1] - residues[0]
    pieces = [len(stream) for stream in streams]
    size = GROUP * len(residues)
    return pl.pallas_call(
        functools.partial(correlate_kernel, n_inp, n_tm, frames, pieces, together, has_base),
        grid=(GROUP // together, len(residues)),
        out_shape=jax.ShapeDtypeStruct((2, GROUP, step, n_inputs, n_inputs), jnp.float32),
        in_specs=specs,
        out_specs=pl.BlockSpec(
            (2, together, 1, n_inputs, n_inputs), lambda c, r: (0, c, residues[0] + gap * r, 0, 0)
        ),
        input_output_aliases=aliases,
        compiler_params=pltpu.CompilerParams(vmem_limit_bytes=VMEM_BYTES),
        cost_estimate=pl.CostEstimate(
            flops=12 * size * n_inputs * n_inputs * n_tm * LANES,
            bytes_accessed=4 * size * (n_inputs * n_tm * LANES + 2 * n_inputs * n_inputs),
            transcendentals=0,
        ),
        name="correlate_" + "_".join(map(str, residues)),
    )(*operands)


def on_device(voltages, filter_taps):
    inputs_dev, frames, nfft = voltages.shape
    n_inp = lax.axis_size("inp")
    n_tm = lax.axis_size("tm")
    count = n_inp * n_tm
    ch_dev = nfft // 2 // count
    step = ch_dev // GROUP
    blocks = inputs_dev // BLOCK

    def history(tail):
        return lax.ppermute(tail, "tm", [(t, t + 1) for t in range(n_tm - 1)])

    def exchange(payload):
        return lax.all_to_all(payload, AXES, split_axis=0, concat_axis=0, tiled=True)

    def spectra(before, residues, half, *places):
        return transform(voltages, before, filter_taps, count, ch_dev, step, residues, half, *places)

    def visibilities(streams, base, residues):
        return correlate(streams, base, n_inp, n_tm, inputs_dev, frames, ch_dev, step, residues)

    everything = (0, blocks)
    if step != 4 or blocks % 4:
        past = filter_taps.shape[0] - 1
        before = history(voltages[:, frames - past :, :].reshape(-1, nfft))
        result = None
        for residue in range(step):
            (sent,) = spectra(before, [residue], None, everything, blocks, 0)
            result = visibilities([[(exchange(sent), blocks, 0)]], result, [residue])
        return result.reshape(2, ch_dev, *result.shape[3:])

    rest = blocks - 1
    first, tail_first = spectra(None, [0, 2], 1, (0, 1), 1, 0)
    got_first = exchange(first)
    second, tail_rest = spectra(None, [0, 2], 1, (1, blocks), rest, 0)
    before = history(jnp.concatenate([tail_first, tail_rest], axis=0))
    got_second = exchange(second)
    (third,) = spectra(before, [0, 2], 0, everything, 2 * blocks, 0)
    (third,) = spectra(before, [1], None, everything, 2 * blocks, blocks, third)
    got_third = exchange(third)
    (fourth,) = spectra(before, [3], None, everything, blocks, 0)
    got_fourth = exchange(fourth)
    late = [(got_first, 1, 0), (got_second, rest, 0)]
    early = [(got_third, blocks, 0)]
    result = visibilities([late, early], None, [0, 2])
    result = visibilities([[(got_third, blocks, blocks)]], result, [1])
    result = visibilities([[(got_fourth, blocks, 0)]], result, [3])
    return result.reshape(2, ch_dev, *result.shape[3:])


def solution(mesh):
    return jax.shard_map(
        on_device,
        mesh=mesh,
        in_specs=(P("inp", "tm", None), P()),
        out_specs=P(None, AXES, None, None),
        check_vma=False,
    )
```

```python
import functools
import math

import jax
import jax.numpy as jnp
import ml_dtypes
import numpy as np
from jax import lax
from jax.experimental import pallas as pl
from jax.experimental.pallas import tpu as pltpu
from jax.sharding import PartitionSpec as P

AXES = ("inp", "tm")
GROUP = 8
BLOCK = 8
ROWS = GROUP * BLOCK
LANES = 128
PAIR = 16
VMEM_BYTES = 56 * 1024 * 1024
NT = (((1,), (1,)), ((), ()))


def fold_of(step, residue):
    if step % 4 == 0 and residue % 4 == 0:
        return "sum4"
    if step % 4 == 0 and residue % 4 == 2:
        return "alt4"
    if step % 2 == 0 and residue % 2 == 1:
        return "diff2"
    return "none"


def fold_terms(nfft, fold):
    return {"sum4": nfft // 4, "alt4": nfft // 4, "diff2": nfft // 2, "none": nfft}[fold]


def transform_table(nfft, ch_dev, count, step, residue):
    depth = fold_terms(nfft, fold_of(step, residue))
    dest = np.arange(count)[:, None]
    channel = dest * ch_dev + step * np.arange(GROUP)[None, :] + residue
    phase = channel[:, :, None] * np.arange(depth)[None, None, :] % nfft
    angle = 2.0 * math.pi / nfft * phase.astype(np.float64)
    scale = 1.0 / math.sqrt(nfft)
    table = np.concatenate([np.cos(angle), -np.sin(angle)], axis=1) * scale
    high = table.astype(ml_dtypes.bfloat16)
    low = (table - high.astype(np.float64)).astype(ml_dtypes.bfloat16)
    return high, low


def split(value):
    high = value.astype(jnp.bfloat16)
    return high, (value - high.astype(jnp.float32)).astype(jnp.bfloat16)


def dot_nt(a, b):
    return lax.dot_general(a, b, dimension_numbers=NT, preferred_element_type=jnp.float32)


def swap_halves(lane, a, b, width):
    first = lane % (2 * width) < width
    return (
        jnp.where(first, a, pltpu.roll(b, width, 1)),
        jnp.where(first, pltpu.roll(a, LANES - width, 1), b),
    )


def transform_kernel(folds, tiles, has_base, splits, taps_ref, before_ref, *rest):
    x_refs, rest = rest[:tiles], rest[tiles:]
    tables, rest = rest[: 2 * len(folds)], rest[2 * len(folds) + has_base :]
    outs, rest = rest[:splits], rest[splits:]
    folded, head = rest[: 2 * len(folds)], rest[2 * len(folds)]
    block, frames, _ = x_refs[0].shape
    count = outs[0].shape[0]
    taps = taps_ref.shape[0]
    past = taps - 1
    quarter = tiles // 4

    def weights(tile):
        columns = slice(tile * LANES, (tile + 1) * LANES)
        return [taps_ref[k : k + 1, columns] for k in range(taps)]

    def fill_head(slot, i, tile):
        columns = slice(tile * LANES, (tile + 1) * LANES)
        if len(before_ref.shape) == 3:
            head[slot, 0:8, :] = before_ref[i, :, columns]
        else:
            for r in range(past):
                row = before_ref[pl.ds(i * past + r, 1), columns]
                head[slot, 8 - past + r : 9 - past + r, :] = row
        head[slot, 8 : 8 + PAIR, :] = x_refs[tile][i, 0:PAIR, :]

    def window(slot, i, tile, start):
        if start < taps:
            return head[slot, pl.ds(8 + start, 8, stride=2), :]
        return x_refs[tile][i, pl.ds(start, 8, stride=2), :]

    def filtered(slot, i, tile, first, tap_rows):
        loads = [window(slot, i, tile, first + 1 - back) for back in range(taps + 1)]
        halves = []
        for odd in (0, 1):
            total = tap_rows[taps - 1] * loads[1 - odd]
            for back in range(1, taps):
                total = total + tap_rows[taps - 1 - back] * loads[1 - odd + back]
            halves.append(total)
        return jnp.concatenate(halves, axis=0)

    def store(which, rows, tile, value):
        high, low = split(value)
        columns = slice(tile * LANES, (tile + 1) * LANES)
        folded[2 * which][rows, columns] = high
        folded[2 * which + 1][rows, columns] = low

    for tile in range(tiles if "none" in folds else quarter):
        sources = [tile] if "none" in folds else [tile + q * quarter for q in range(4)]

        @pl.loop(0, block, unroll=block)
        def _(i):
            tap_rows = [weights(source) for source in sources]
            for slot, source in enumerate(sources):
                fill_head(slot, i, source)
            for first in range(0, frames, PAIR):
                rows = pl.ds(pl.multiple_of(i * frames + first, PAIR), PAIR)
                f = [
                    filtered(slot, i, source, first, tap_rows[slot])
                    for slot, source in enumerate(sources)
                ]
                for which, fold in enumerate(folds):
                    if fold == "none":
                        store(which, rows, tile, f[0])
                    elif fold == "sum4":
                        store(which, rows, tile, (f[0] + f[2]) + (f[1] + f[3]))
                    elif fold == "alt4":
                        store(which, rows, tile, (f[0] + f[2]) - (f[1] + f[3]))
                    else:
                        store(which, rows, tile, f[0] - f[2])
                        store(which, rows, tile + quarter, f[1] - f[3])

    lane = lax.broadcasted_iota(jnp.int32, (GROUP, LANES), 1)
    together = min(16, count)
    for start in range(0, count, together):
        rows = slice(start * 2 * GROUP, (start + together) * 2 * GROUP)
        specs = []
        for which in range(len(folds)):
            a_hi, a_lo = tables[2 * which][rows], tables[2 * which + 1][rows]
            g_hi, g_lo = folded[2 * which], folded[2 * which + 1]
            specs.append(dot_nt(a_hi, g_hi[...]) + dot_nt(a_lo, g_hi[...]) + dot_nt(a_hi, g_lo[...]))
        for k in range(together):
            top = 2 * GROUP * k
            parts = [s[top + h * GROUP : top + (h + 1) * GROUP] for s in specs for h in (0, 1)]
            for at in range(0, block * frames // LANES):
                tiles_at = [p[:, at * LANES : (at + 1) * LANES] for p in parts]
                if len(parts) == 2:
                    mixed = swap_halves(lane, tiles_at[0], tiles_at[1], LANES // 2)
                else:
                    u0, u2 = swap_halves(lane, tiles_at[0], tiles_at[2], LANES // 2)
                    u1, u3 = swap_halves(lane, tiles_at[1], tiles_at[3], LANES // 2)
                    mixed = swap_halves(lane, u0, u1, LANES // 4) + swap_halves(lane, u2, u3, LANES // 4)
                for j, tile in enumerate(mixed):
                    i = at * len(parts) + j
                    share = GROUP // splits
                    for n, out in enumerate(outs):
                        rows = pl.ds(i, share, stride=block)
                        out[start + k, rows, :] = tile[n * share : (n + 1) * share]


def last_frames_kernel(past, x_ref, _, out):
    inputs_dev, rows, _ = x_ref.shape
    for i in range(inputs_dev):
        for r in range(past):
            out[i * past + r : i * past + r + 1, :] = x_ref[i, rows - past + r : rows - past + r + 1, :]


def last_frames(voltages, past, event):
    inputs_dev, frames, nfft = voltages.shape
    return pl.pallas_call(
        functools.partial(last_frames_kernel, past),
        grid=(1,),
        out_shape=jax.ShapeDtypeStruct((inputs_dev * past, nfft), jnp.float32),
        in_specs=[
            pl.BlockSpec((inputs_dev, 8, nfft), lambda b: (0, frames // 8 - 1, 0)),
            pl.BlockSpec(memory_space=pl.ANY),
        ],
        out_specs=pl.BlockSpec((inputs_dev * past, nfft), lambda b: (0, 0)),
        compiler_params=pltpu.CompilerParams(vmem_limit_bytes=VMEM_BYTES),
        name="last_frames",
    )(voltages, event)


def transform(voltages, before, filter_taps, count, ch_dev, step, residues, half, span, *places):
    inputs_dev, frames, nfft = voltages.shape
    past = filter_taps.shape[0] - 1
    folds = [fold_of(step, residue) for residue in residues]
    tiles = nfft // LANES
    if half is not None:
        frames = frames // 2
    low, high = span
    blocks = high - low
    base = places[0][2] if len(places[0]) == 3 else None
    has_base = int(base is not None)
    operands = []
    specs = []

    def add(operand, spec):
        operands.append(operand)
        specs.append(spec)

    add(filter_taps, pl.BlockSpec(filter_taps.shape, lambda b: (0, 0)))
    if half == 1:
        add(voltages, pl.BlockSpec((BLOCK, 8, nfft), lambda b: (b + low, frames // 8 - 1, 0)))
    else:
        add(before, pl.BlockSpec((BLOCK * past, nfft), lambda b: (b + low, 0)))
    for tile in range(tiles):
        add(voltages, pl.BlockSpec((BLOCK, frames, LANES), lambda b, t=tile: (b + low, half or 0, t)))
    scratch = []
    flops = 0
    for residue, fold in zip(residues, folds):
        depth = fold_terms(nfft, fold)
        for table in transform_table(nfft, ch_dev, count, step, residue):
            table = table.reshape(-1, depth)
            add(
                jnp.asarray(table),
                pl.BlockSpec(table.shape, lambda b: (0, 0), pipeline_mode=pl.Buffered(1)),
            )
        scratch += [pltpu.VMEM((BLOCK * frames, depth), jnp.bfloat16)] * 2
        flops += 6 * 2 * GROUP * count * depth * blocks * BLOCK * frames
    scratch.append(pltpu.VMEM((4, 8 + PAIR, LANES), jnp.float32))
    aliases = {}
    if has_base:
        aliases[len(operands)] = 0
        add(base, pl.BlockSpec(memory_space=pl.ANY))
    share = ROWS // len(places)
    return pl.pallas_call(
        functools.partial(transform_kernel, folds, tiles, has_base, len(places)),
        grid=(blocks,),
        out_shape=[jax.ShapeDtypeStruct((count, place[0] * share, LANES), jnp.float32) for place in places],
        input_output_aliases=aliases,
        in_specs=specs,
        out_specs=[
            pl.BlockSpec((count, share, LANES), lambda b, at=place[1]: (0, b + at, 0)) for place in places
        ],
        scratch_shapes=scratch,
        compiler_params=pltpu.CompilerParams(vmem_limit_bytes=VMEM_BYTES),
        cost_estimate=pl.CostEstimate(
            flops=flops, bytes_accessed=4 * blocks * BLOCK * frames * nfft, transcendentals=0
        ),
        name="spectra_" + "_".join(map(str, residues)) + ("" if half is None else f"_half{half}"),
    )(*operands)


def correlate_kernel(n_inp, n_tm, frames, pieces, together, has_base, *rest):
    streams = []
    for number in pieces:
        streams.append(rest[:number])
        rest = rest[number:]
    (out,) = rest[has_base:]
    scale = 1.0 / (n_tm * frames)
    width = LANES // 2 // len(pieces)
    first = lax.broadcasted_iota(jnp.int32, (1, LANES), 1) % (2 * width) < width
    low_half = lax.broadcasted_iota(jnp.int32, (1, LANES), 1) < LANES // 2

    def payload(stream, sender, c):
        rows = slice(c * BLOCK, (c + 1) * BLOCK)
        return [
            array[sender, b, rows, :] for array in streams[stream] for b in range(array.shape[1])
        ]

    for c in range(together):
        columns = []
        for t in range(n_tm):
            senders = [p * n_tm + t for p in range(n_inp)]
            value = jnp.concatenate([x for s in senders for x in payload(0, s, c)], axis=0)
            if len(pieces) == 1:
                turned = pltpu.roll(value, width, 1)
                turned = jnp.where(first, turned, -turned)
            else:
                other = jnp.concatenate([x for s in senders for x in payload(1, s, c)], axis=0)
                turn = pl.program_id(1) * (LANES // 2)
                value = jnp.where(
                    low_half, pltpu.roll(value, turn, 1), pltpu.roll(other, LANES // 2 - turn, 1)
                )
                turned = jnp.where(
                    first, pltpu.roll(value, LANES - width, 1), -pltpu.roll(value, width, 1)
                )
            columns.append(split(value) + split(turned))
        p_hi, p_lo, t_hi, t_lo = [jnp.concatenate(column, axis=1) for column in zip(*columns)]
        right = jnp.concatenate([p_hi, p_hi, p_lo], axis=1)
        out[0, c, 0] = dot_nt(jnp.concatenate([p_hi, p_lo, p_hi], axis=1), right) * scale
        out[1, c, 0] = dot_nt(jnp.concatenate([t_hi, t_lo, t_hi], axis=1), right) * scale


def correlate(streams, base, n_inp, n_tm, inputs_dev, frames, ch_dev, step, residues, channels):
    count = n_inp * n_tm
    n_inputs = n_inp * inputs_dev
    has_base = int(base is not None)
    together = 2
    operands = []
    specs = []
    for stream in streams:
        for array, number, at in stream:
            operands.append(array.reshape(count, -1, (channels[1] - channels[0]) * BLOCK, LANES))
            specs.append(
                pl.BlockSpec(
                    (count, number, together * BLOCK, LANES),
                    lambda c, r, q=at // number: (0, q, c, 0),
                )
            )
    aliases = {}
    if has_base:
        aliases[len(operands)] = 0
        operands.append(base)
        specs.append(pl.BlockSpec(memory_space=pl.ANY))
    gap = residues[-1] - residues[0]
    pieces = [len(stream) for stream in streams]
    size = (channels[1] - channels[0]) * len(residues)
    skip = channels[0] // together
    return pl.pallas_call(
        functools.partial(correlate_kernel, n_inp, n_tm, frames, pieces, together, has_base),
        grid=((channels[1] - channels[0]) // together, len(residues)),
        out_shape=jax.ShapeDtypeStruct((2, GROUP, step, n_inputs, n_inputs), jnp.float32),
        in_specs=specs,
        out_specs=pl.BlockSpec(
            (2, together, 1, n_inputs, n_inputs), lambda c, r: (0, c + skip, residues[0] + gap * r, 0, 0)
        ),
        input_output_aliases=aliases,
        compiler_params=pltpu.CompilerParams(vmem_limit_bytes=62 * 1024 * 1024),
        cost_estimate=pl.CostEstimate(
            flops=12 * size * n_inputs * n_inputs * n_tm * LANES,
            bytes_accessed=4 * size * (n_inputs * n_tm * LANES + 2 * n_inputs * n_inputs),
            transcendentals=0,
        ),
        name="correlate_" + "_".join(map(str, residues)) + f"_from{channels[0]}",
    )(*operands)


def on_device(voltages, filter_taps):
    inputs_dev, frames, nfft = voltages.shape
    n_inp = lax.axis_size("inp")
    n_tm = lax.axis_size("tm")
    count = n_inp * n_tm
    ch_dev = nfft // 2 // count
    step = ch_dev // GROUP
    blocks = inputs_dev // BLOCK

    def history(tail):
        return lax.ppermute(tail, "tm", [(t, t + 1) for t in range(n_tm - 1)])

    def exchange(payload):
        return lax.all_to_all(payload, AXES, split_axis=0, concat_axis=0, tiled=True)

    def spectra(before, residues, half, *places):
        return transform(voltages, before, filter_taps, count, ch_dev, step, residues, half, *places)

    def visibilities(streams, base, residues, channels=(0, GROUP)):
        return correlate(
            streams, base, n_inp, n_tm, inputs_dev, frames, ch_dev, step, residues, channels
        )

    everything = (0, blocks)
    if step != 4 or blocks % 4:
        past = filter_taps.shape[0] - 1
        before = history(voltages[:, frames - past :, :].reshape(-1, nfft))
        result = None
        for residue in range(step):
            (sent,) = spectra(before, [residue], None, everything, (blocks, 0))
            result = visibilities([[(exchange(sent), blocks, 0)]], result, [residue])
        return result.reshape(2, ch_dev, *result.shape[3:])

    (first,) = spectra(None, [0, 2], 1, everything, (blocks, 0))
    got_first = exchange(first)
    before = history(last_frames(voltages, filter_taps.shape[0] - 1, first))
    size = 2 * blocks + blocks // 2
    (second,) = spectra(before, [0, 2], 0, everything, (size, 0))
    (second,) = spectra(before, [1], None, everything, (size, blocks, second))
    second, third = spectra(before, [3], None, everything, (2 * size, 4 * blocks, second), (blocks, 0))
    got_second = exchange(second)
    got_third = exchange(third)
    streams = [[(got_first, blocks, 0)], [(got_second, blocks, 0)]]
    result = visibilities(streams, None, [0, 2])
    result = visibilities([[(got_second, blocks, blocks)]], result, [1])
    result = visibilities([[(got_second, blocks, 4 * blocks)]], result, [3], (0, GROUP // 2))
    result = visibilities([[(got_third, blocks, 0)]], result, [3], (GROUP // 2, GROUP))
    return result.reshape(2, ch_dev, *result.shape[3:])


def solution(mesh):
    return jax.shard_map(
        on_device,
        mesh=mesh,
        in_specs=(P("inp", "tm", None), P()),
        out_specs=P(None, AXES, None, None),
        check_vma=False,
    )
```

```python
import functools
import math

import jax
import jax.numpy as jnp
import ml_dtypes
import numpy as np
from jax import lax
from jax.experimental import pallas as pl
from jax.experimental.pallas import tpu as pltpu
from jax.sharding import PartitionSpec as P

AXES = ("inp", "tm")
GROUP = 8
BLOCK = 8
ROWS = GROUP * BLOCK
LANES = 128
PAIR = 16
VMEM_BYTES = 56 * 1024 * 1024
NT = (((1,), (1,)), ((), ()))


def fold_of(step, residue):
    if step % 4 == 0 and residue % 4 == 0:
        return "sum4"
    if step % 4 == 0 and residue % 4 == 2:
        return "alt4"
    if step % 2 == 0 and residue % 2 == 1:
        return "diff2"
    return "none"


def fold_terms(nfft, fold):
    return {"sum4": nfft // 4, "alt4": nfft // 4, "diff2": nfft // 2, "none": nfft}[fold]


def transform_table(nfft, ch_dev, count, step, residue):
    depth = fold_terms(nfft, fold_of(step, residue))
    dest = np.arange(count)[:, None]
    channel = dest * ch_dev + step * np.arange(GROUP)[None, :] + residue
    phase = channel[:, :, None] * np.arange(depth)[None, None, :] % nfft
    angle = 2.0 * math.pi / nfft * phase.astype(np.float64)
    scale = 1.0 / math.sqrt(nfft)
    table = np.concatenate([np.cos(angle), -np.sin(angle)], axis=1) * scale
    high = table.astype(ml_dtypes.bfloat16)
    low = (table - high.astype(np.float64)).astype(ml_dtypes.bfloat16)
    return high, low


def split(value):
    high = value.astype(jnp.bfloat16)
    return high, (value - high.astype(jnp.float32)).astype(jnp.bfloat16)


def dot_nt(a, b):
    return lax.dot_general(a, b, dimension_numbers=NT, preferred_element_type=jnp.float32)


def swap_halves(lane, a, b, width):
    first = lane % (2 * width) < width
    return (
        jnp.where(first, a, pltpu.roll(b, width, 1)),
        jnp.where(first, pltpu.roll(a, LANES - width, 1), b),
    )


def transform_kernel(folds, tiles, has_base, splits, taps_ref, before_ref, *rest):
    x_refs, rest = rest[:tiles], rest[tiles:]
    tables, rest = rest[: 2 * len(folds)], rest[2 * len(folds) + has_base :]
    outs, rest = rest[:splits], rest[splits:]
    folded, head = rest[: 2 * len(folds)], rest[2 * len(folds)]
    block, frames, _ = x_refs[0].shape
    count = outs[0].shape[0]
    taps = taps_ref.shape[0]
    past = taps - 1
    quarter = tiles // 4

    def weights(tile):
        columns = slice(tile * LANES, (tile + 1) * LANES)
        return [taps_ref[k : k + 1, columns] for k in range(taps)]

    def fill_head(slot, i, tile):
        columns = slice(tile * LANES, (tile + 1) * LANES)
        if len(before_ref.shape) == 3:
            head[slot, 0:8, :] = before_ref[i, :, columns]
        else:
            for r in range(past):
                row = before_ref[pl.ds(i * past + r, 1), columns]
                head[slot, 8 - past + r : 9 - past + r, :] = row
        head[slot, 8 : 8 + PAIR, :] = x_refs[tile][i, 0:PAIR, :]

    def window(slot, i, tile, start):
        if start < taps:
            return head[slot, pl.ds(8 + start, 8, stride=2), :]
        return x_refs[tile][i, pl.ds(start, 8, stride=2), :]

    def filtered(slot, i, tile, first, tap_rows):
        loads = [window(slot, i, tile, first + 1 - back) for back in range(taps + 1)]
        halves = []
        for odd in (0, 1):
            total = tap_rows[taps - 1] * loads[1 - odd]
            for back in range(1, taps):
                total = total + tap_rows[taps - 1 - back] * loads[1 - odd + back]
            halves.append(total)
        return jnp.concatenate(halves, axis=0)

    def store(which, rows, tile, value):
        high, low = split(value)
        columns = slice(tile * LANES, (tile + 1) * LANES)
        folded[2 * which][rows, columns] = high
        folded[2 * which + 1][rows, columns] = low

    for tile in range(tiles if "none" in folds else quarter):
        sources = [tile] if "none" in folds else [tile + q * quarter for q in range(4)]

        @pl.loop(0, block, unroll=block)
        def _(i):
            tap_rows = [weights(source) for source in sources]
            for slot, source in enumerate(sources):
                fill_head(slot, i, source)
            for first in range(0, frames, PAIR):
                rows = pl.ds(pl.multiple_of(i * frames + first, PAIR), PAIR)
                f = [
                    filtered(slot, i, source, first, tap_rows[slot])
                    for slot, source in enumerate(sources)
                ]
                for which, fold in enumerate(folds):
                    if fold == "none":
                        store(which, rows, tile, f[0])
                    elif fold == "sum4":
                        store(which, rows, tile, (f[0] + f[2]) + (f[1] + f[3]))
                    elif fold == "alt4":
                        store(which, rows, tile, (f[0] + f[2]) - (f[1] + f[3]))
                    else:
                        store(which, rows, tile, f[0] - f[2])
                        store(which, rows, tile + quarter, f[1] - f[3])

    lane = lax.broadcasted_iota(jnp.int32, (GROUP, LANES), 1)
    together = min(16, count)
    for start in range(0, count, together):
        rows = slice(start * 2 * GROUP, (start + together) * 2 * GROUP)
        specs = []
        for which in range(len(folds)):
            a_hi, a_lo = tables[2 * which][rows], tables[2 * which + 1][rows]
            g_hi, g_lo = folded[2 * which], folded[2 * which + 1]
            specs.append(dot_nt(a_hi, g_hi[...]) + dot_nt(a_lo, g_hi[...]) + dot_nt(a_hi, g_lo[...]))
        for k in range(together):
            top = 2 * GROUP * k
            parts = [s[top + h * GROUP : top + (h + 1) * GROUP] for s in specs for h in (0, 1)]
            for at in range(0, block * frames // LANES):
                tiles_at = [p[:, at * LANES : (at + 1) * LANES] for p in parts]
                if len(parts) == 2:
                    mixed = swap_halves(lane, tiles_at[0], tiles_at[1], LANES // 2)
                else:
                    u0, u2 = swap_halves(lane, tiles_at[0], tiles_at[2], LANES // 2)
                    u1, u3 = swap_halves(lane, tiles_at[1], tiles_at[3], LANES // 2)
                    mixed = swap_halves(lane, u0, u1, LANES // 4) + swap_halves(lane, u2, u3, LANES // 4)
                for j, tile in enumerate(mixed):
                    i = at * len(parts) + j
                    share = GROUP // splits
                    for n, out in enumerate(outs):
                        rows = pl.ds(i, share, stride=block)
                        out[start + k, rows, :] = tile[n * share : (n + 1) * share]


def last_frames_kernel(past, x_ref, _, out):
    inputs_dev, rows, _ = x_ref.shape
    for i in range(inputs_dev):
        for r in range(past):
            out[i * past + r : i * past + r + 1, :] = x_ref[i, rows - past + r : rows - past + r + 1, :]


def last_frames(voltages, past, event):
    inputs_dev, frames, nfft = voltages.shape
    return pl.pallas_call(
        functools.partial(last_frames_kernel, past),
        grid=(1,),
        out_shape=jax.ShapeDtypeStruct((inputs_dev * past, nfft), jnp.float32),
        in_specs=[
            pl.BlockSpec((inputs_dev, 8, nfft), lambda b: (0, frames // 8 - 1, 0)),
            pl.BlockSpec(memory_space=pl.ANY),
        ],
        out_specs=pl.BlockSpec((inputs_dev * past, nfft), lambda b: (0, 0)),
        compiler_params=pltpu.CompilerParams(vmem_limit_bytes=VMEM_BYTES),
        name="last_frames",
    )(voltages, event)


def transform(voltages, before, filter_taps, count, ch_dev, step, residues, half, span, *places):
    inputs_dev, frames, nfft = voltages.shape
    past = filter_taps.shape[0] - 1
    folds = [fold_of(step, residue) for residue in residues]
    tiles = nfft // LANES
    if half is not None:
        frames = frames // 2
    low, high = span
    blocks = high - low
    base = places[0][2] if len(places[0]) == 3 else None
    has_base = int(base is not None)
    operands = []
    specs = []

    def add(operand, spec):
        operands.append(operand)
        specs.append(spec)

    add(filter_taps, pl.BlockSpec(filter_taps.shape, lambda b: (0, 0)))
    if half == 1:
        add(voltages, pl.BlockSpec((BLOCK, 8, nfft), lambda b: (b + low, frames // 8 - 1, 0)))
    else:
        add(before, pl.BlockSpec((BLOCK * past, nfft), lambda b: (b + low, 0)))
    for tile in range(tiles):
        add(voltages, pl.BlockSpec((BLOCK, frames, LANES), lambda b, t=tile: (b + low, half or 0, t)))
    scratch = []
    flops = 0
    for residue, fold in zip(residues, folds):
        depth = fold_terms(nfft, fold)
        for table in transform_table(nfft, ch_dev, count, step, residue):
            table = table.reshape(-1, depth)
            add(
                jnp.asarray(table),
                pl.BlockSpec(table.shape, lambda b: (0, 0), pipeline_mode=pl.Buffered(1)),
            )
        scratch += [pltpu.VMEM((BLOCK * frames, depth), jnp.bfloat16)] * 2
        flops += 6 * 2 * GROUP * count * depth * blocks * BLOCK * frames
    scratch.append(pltpu.VMEM((4, 8 + PAIR, LANES), jnp.float32))
    aliases = {}
    if has_base:
        aliases[len(operands)] = 0
        add(base, pl.BlockSpec(memory_space=pl.ANY))
    share = ROWS // len(places)
    return pl.pallas_call(
        functools.partial(transform_kernel, folds, tiles, has_base, len(places)),
        grid=(blocks,),
        out_shape=[jax.ShapeDtypeStruct((count, place[0] * share, LANES), jnp.float32) for place in places],
        input_output_aliases=aliases,
        in_specs=specs,
        out_specs=[
            pl.BlockSpec((count, share, LANES), lambda b, at=place[1]: (0, b + at, 0)) for place in places
        ],
        scratch_shapes=scratch,
        compiler_params=pltpu.CompilerParams(vmem_limit_bytes=VMEM_BYTES),
        cost_estimate=pl.CostEstimate(
            flops=flops, bytes_accessed=4 * blocks * BLOCK * frames * nfft, transcendentals=0
        ),
        name="spectra_" + "_".join(map(str, residues)) + ("" if half is None else f"_half{half}"),
    )(*operands)


def correlate_kernel(n_inp, n_tm, frames, pieces, together, has_base, *rest):
    streams = []
    for number in pieces:
        streams.append(rest[:number])
        rest = rest[number:]
    (out,) = rest[has_base:]
    scale = 1.0 / (n_tm * frames)
    width = LANES // 2 // len(pieces)
    first = lax.broadcasted_iota(jnp.int32, (1, LANES), 1) % (2 * width) < width
    low_half = lax.broadcasted_iota(jnp.int32, (1, LANES), 1) < LANES // 2

    def payload(stream, sender, c):
        rows = slice(c * BLOCK, (c + 1) * BLOCK)
        return [
            array[sender, b, rows, :] for array in streams[stream] for b in range(array.shape[1])
        ]

    for c in range(together):
        columns = []
        for t in range(n_tm):
            senders = [p * n_tm + t for p in range(n_inp)]
            value = jnp.concatenate([x for s in senders for x in payload(0, s, c)], axis=0)
            if len(pieces) == 1:
                turned = pltpu.roll(value, width, 1)
                turned = jnp.where(first, turned, -turned)
            else:
                other = jnp.concatenate([x for s in senders for x in payload(1, s, c)], axis=0)
                turn = pl.program_id(1) * (LANES // 2)
                value = jnp.where(
                    low_half, pltpu.roll(value, turn, 1), pltpu.roll(other, LANES // 2 - turn, 1)
                )
                turned = jnp.where(
                    first, pltpu.roll(value, LANES - width, 1), -pltpu.roll(value, width, 1)
                )
            columns.append(split(value) + (turned.astype(jnp.bfloat16),))
        p_hi, p_lo, t_hi = [jnp.concatenate(column, axis=1) for column in zip(*columns)]
        plain = dot_nt(p_hi, p_lo)
        twist = dot_nt(t_hi, p_lo)
        out[0, c, 0] = (dot_nt(p_hi, p_hi) + (plain + plain.T)) * scale
        out[1, c, 0] = (dot_nt(t_hi, p_hi) + (twist - twist.T)) * scale


def correlate(streams, base, n_inp, n_tm, inputs_dev, frames, ch_dev, step, residues, channels):
    count = n_inp * n_tm
    n_inputs = n_inp * inputs_dev
    has_base = int(base is not None)
    together = 2
    operands = []
    specs = []
    for stream in streams:
        for array, number, at in stream:
            operands.append(array.reshape(count, -1, (channels[1] - channels[0]) * BLOCK, LANES))
            specs.append(
                pl.BlockSpec(
                    (count, number, together * BLOCK, LANES),
                    lambda c, r, q=at // number: (0, q, c, 0),
                )
            )
    aliases = {}
    if has_base:
        aliases[len(operands)] = 0
        operands.append(base)
        specs.append(pl.BlockSpec(memory_space=pl.ANY))
    gap = residues[-1] - residues[0]
    pieces = [len(stream) for stream in streams]
    size = (channels[1] - channels[0]) * len(residues)
    skip = channels[0] // together
    return pl.pallas_call(
        functools.partial(correlate_kernel, n_inp, n_tm, frames, pieces, together, has_base),
        grid=((channels[1] - channels[0]) // together, len(residues)),
        out_shape=jax.ShapeDtypeStruct((2, GROUP, step, n_inputs, n_inputs), jnp.float32),
        in_specs=specs,
        out_specs=pl.BlockSpec(
            (2, together, 1, n_inputs, n_inputs), lambda c, r: (0, c + skip, residues[0] + gap * r, 0, 0)
        ),
        input_output_aliases=aliases,
        compiler_params=pltpu.CompilerParams(vmem_limit_bytes=62 * 1024 * 1024),
        cost_estimate=pl.CostEstimate(
            flops=12 * size * n_inputs * n_inputs * n_tm * LANES,
            bytes_accessed=4 * size * (n_inputs * n_tm * LANES + 2 * n_inputs * n_inputs),
            transcendentals=0,
        ),
        name="correlate_" + "_".join(map(str, residues)) + f"_from{channels[0]}",
    )(*operands)


def on_device(voltages, filter_taps):
    inputs_dev, frames, nfft = voltages.shape
    n_inp = lax.axis_size("inp")
    n_tm = lax.axis_size("tm")
    count = n_inp * n_tm
    ch_dev = nfft // 2 // count
    step = ch_dev // GROUP
    blocks = inputs_dev // BLOCK

    def history(tail):
        return lax.ppermute(tail, "tm", [(t, t + 1) for t in range(n_tm - 1)])

    def exchange(payload):
        return lax.all_to_all(payload, AXES, split_axis=0, concat_axis=0, tiled=True)

    def spectra(before, residues, half, *places):
        return transform(voltages, before, filter_taps, count, ch_dev, step, residues, half, *places)

    def visibilities(streams, base, residues, channels=(0, GROUP)):
        return correlate(
            streams, base, n_inp, n_tm, inputs_dev, frames, ch_dev, step, residues, channels
        )

    everything = (0, blocks)
    if step != 4 or blocks % 4:
        past = filter_taps.shape[0] - 1
        before = history(voltages[:, frames - past :, :].reshape(-1, nfft))
        result = None
        for residue in range(step):
            (sent,) = spectra(before, [residue], None, everything, (blocks, 0))
            result = visibilities([[(exchange(sent), blocks, 0)]], result, [residue])
        return result.reshape(2, ch_dev, *result.shape[3:])

    (first,) = spectra(None, [0, 2], 1, everything, (blocks, 0))
    got_first = exchange(first)
    before = history(last_frames(voltages, filter_taps.shape[0] - 1, first))
    size = 2 * blocks + blocks // 2
    (second,) = spectra(before, [0, 2], 0, everything, (size, 0))
    (second,) = spectra(before, [1], None, everything, (size, blocks, second))
    second, third = spectra(before, [3], None, everything, (2 * size, 4 * blocks, second), (blocks, 0))
    got_second = exchange(second)
    got_third = exchange(third)
    streams = [[(got_first, blocks, 0)], [(got_second, blocks, 0)]]
    result = visibilities(streams, None, [0, 2])
    result = visibilities([[(got_second, blocks, blocks)]], result, [1])
    result = visibilities([[(got_second, blocks, 4 * blocks)]], result, [3], (0, GROUP // 2))
    result = visibilities([[(got_third, blocks, 0)]], result, [3], (GROUP // 2, GROUP))
    return result.reshape(2, ch_dev, *result.shape[3:])


def solution(mesh):
    return jax.shard_map(
        on_device,
        mesh=mesh,
        in_specs=(P("inp", "tm", None), P()),
        out_specs=P(None, AXES, None, None),
        check_vma=False,
    )
```

```python
import functools
import math

import jax
import jax.numpy as jnp
import ml_dtypes
import numpy as np
from jax import lax
from jax.experimental import pallas as pl
from jax.experimental.pallas import tpu as pltpu
from jax.sharding import PartitionSpec as P

AXES = ("inp", "tm")
GROUP = 8
BLOCK = 8
ROWS = GROUP * BLOCK
LANES = 128
PAIR = 16
VMEM_BYTES = 56 * 1024 * 1024
NT = (((1,), (1,)), ((), ()))


def fold_of(step, residue):
    if step % 4 == 0 and residue % 4 == 0:
        return "sum4"
    if step % 4 == 0 and residue % 4 == 2:
        return "alt4"
    if step % 2 == 0 and residue % 2 == 1:
        return "diff2"
    return "none"


def fold_terms(nfft, fold):
    return {"sum4": nfft // 4, "alt4": nfft // 4, "diff2": nfft // 2, "none": nfft}[fold]


def transform_table(nfft, ch_dev, count, step, residue):
    depth = fold_terms(nfft, fold_of(step, residue))
    dest = np.arange(count)[:, None]
    channel = dest * ch_dev + step * np.arange(GROUP)[None, :] + residue
    phase = channel[:, :, None] * np.arange(depth)[None, None, :] % nfft
    angle = 2.0 * math.pi / nfft * phase.astype(np.float64)
    scale = 1.0 / math.sqrt(nfft)
    table = np.concatenate([np.cos(angle), -np.sin(angle)], axis=1) * scale
    high = table.astype(ml_dtypes.bfloat16)
    low = (table - high.astype(np.float64)).astype(ml_dtypes.bfloat16)
    return high, low


def split(value):
    high = value.astype(jnp.bfloat16)
    return high, (value - high.astype(jnp.float32)).astype(jnp.bfloat16)


def dot_nt(a, b):
    return lax.dot_general(a, b, dimension_numbers=NT, preferred_element_type=jnp.float32)


def swap_halves(lane, a, b, width):
    first = lane % (2 * width) < width
    return (
        jnp.where(first, a, pltpu.roll(b, width, 1)),
        jnp.where(first, pltpu.roll(a, LANES - width, 1), b),
    )


def transform_kernel(folds, tiles, has_base, splits, taps_ref, before_ref, *rest):
    x_refs, rest = rest[:tiles], rest[tiles:]
    tables, rest = rest[: 2 * len(folds)], rest[2 * len(folds) + has_base :]
    outs, rest = rest[:splits], rest[splits:]
    folded, head = rest[: 2 * len(folds)], rest[2 * len(folds)]
    block, frames, _ = x_refs[0].shape
    count = outs[0].shape[0]
    taps = taps_ref.shape[0]
    past = taps - 1
    quarter = tiles // 4

    def weights(tile):
        columns = slice(tile * LANES, (tile + 1) * LANES)
        return [taps_ref[k : k + 1, columns] for k in range(taps)]

    def fill_head(slot, i, tile):
        columns = slice(tile * LANES, (tile + 1) * LANES)
        if len(before_ref.shape) == 3:
            head[slot, 0:8, :] = before_ref[i, :, columns]
        else:
            for r in range(past):
                row = before_ref[pl.ds(i * past + r, 1), columns]
                head[slot, 8 - past + r : 9 - past + r, :] = row
        head[slot, 8 : 8 + PAIR, :] = x_refs[tile][i, 0:PAIR, :]

    def window(slot, i, tile, start):
        if start < taps:
            return head[slot, pl.ds(8 + start, 8, stride=2), :]
        return x_refs[tile][i, pl.ds(start, 8, stride=2), :]

    def filtered(slot, i, tile, first, tap_rows):
        loads = [window(slot, i, tile, first + 1 - back) for back in range(taps + 1)]
        halves = []
        for odd in (0, 1):
            total = tap_rows[taps - 1] * loads[1 - odd]
            for back in range(1, taps):
                total = total + tap_rows[taps - 1 - back] * loads[1 - odd + back]
            halves.append(total)
        return jnp.concatenate(halves, axis=0)

    def store(which, rows, tile, value):
        high, low = split(value)
        columns = slice(tile * LANES, (tile + 1) * LANES)
        folded[2 * which][rows, columns] = high
        folded[2 * which + 1][rows, columns] = low

    for tile in range(tiles if "none" in folds else quarter):
        sources = [tile] if "none" in folds else [tile + q * quarter for q in range(4)]

        @pl.loop(0, block, unroll=block)
        def _(i):
            tap_rows = [weights(source) for source in sources]
            for slot, source in enumerate(sources):
                fill_head(slot, i, source)
            for first in range(0, frames, PAIR):
                rows = pl.ds(pl.multiple_of(i * frames + first, PAIR), PAIR)
                f = [
                    filtered(slot, i, source, first, tap_rows[slot])
                    for slot, source in enumerate(sources)
                ]
                for which, fold in enumerate(folds):
                    if fold == "none":
                        store(which, rows, tile, f[0])
                    elif fold == "sum4":
                        store(which, rows, tile, (f[0] + f[2]) + (f[1] + f[3]))
                    elif fold == "alt4":
                        store(which, rows, tile, (f[0] + f[2]) - (f[1] + f[3]))
                    else:
                        store(which, rows, tile, f[0] - f[2])
                        store(which, rows, tile + quarter, f[1] - f[3])

    lane = lax.broadcasted_iota(jnp.int32, (GROUP, LANES), 1)
    together = min(16, count)
    for start in range(0, count, together):
        rows = slice(start * 2 * GROUP, (start + together) * 2 * GROUP)
        specs = []
        for which in range(len(folds)):
            a_hi, a_lo = tables[2 * which][rows], tables[2 * which + 1][rows]
            g_hi, g_lo = folded[2 * which], folded[2 * which + 1]
            specs.append(dot_nt(a_hi, g_hi[...]) + dot_nt(a_lo, g_hi[...]) + dot_nt(a_hi, g_lo[...]))
        for k in range(together):
            top = 2 * GROUP * k
            parts = [s[top + h * GROUP : top + (h + 1) * GROUP] for s in specs for h in (0, 1)]
            for at in range(0, block * frames // LANES):
                tiles_at = [p[:, at * LANES : (at + 1) * LANES] for p in parts]
                if len(parts) == 2:
                    mixed = swap_halves(lane, tiles_at[0], tiles_at[1], LANES // 2)
                else:
                    u0, u2 = swap_halves(lane, tiles_at[0], tiles_at[2], LANES // 2)
                    u1, u3 = swap_halves(lane, tiles_at[1], tiles_at[3], LANES // 2)
                    mixed = swap_halves(lane, u0, u1, LANES // 4) + swap_halves(lane, u2, u3, LANES // 4)
                for j, tile in enumerate(mixed):
                    i = at * len(parts) + j
                    share = GROUP // splits
                    for n, out in enumerate(outs):
                        rows = pl.ds(i, share, stride=block)
                        out[start + k, rows, :] = tile[n * share : (n + 1) * share]


def last_frames_kernel(past, x_ref, _, out):
    inputs_dev, rows, _ = x_ref.shape
    for i in range(inputs_dev):
        for r in range(past):
            out[i * past + r : i * past + r + 1, :] = x_ref[i, rows - past + r : rows - past + r + 1, :]


def last_frames(voltages, past, event):
    inputs_dev, frames, nfft = voltages.shape
    return pl.pallas_call(
        functools.partial(last_frames_kernel, past),
        grid=(1,),
        out_shape=jax.ShapeDtypeStruct((inputs_dev * past, nfft), jnp.float32),
        in_specs=[
            pl.BlockSpec((inputs_dev, 8, nfft), lambda b: (0, frames // 8 - 1, 0)),
            pl.BlockSpec(memory_space=pl.ANY),
        ],
        out_specs=pl.BlockSpec((inputs_dev * past, nfft), lambda b: (0, 0)),
        compiler_params=pltpu.CompilerParams(vmem_limit_bytes=VMEM_BYTES),
        name="last_frames",
    )(voltages, event)


def transform(voltages, before, filter_taps, count, ch_dev, step, residues, half, span, *places):
    inputs_dev, frames, nfft = voltages.shape
    past = filter_taps.shape[0] - 1
    folds = [fold_of(step, residue) for residue in residues]
    tiles = nfft // LANES
    if half is not None:
        frames = frames // 2
    low, high = span
    blocks = high - low
    base = places[0][2] if len(places[0]) == 3 else None
    has_base = int(base is not None)
    operands = []
    specs = []

    def add(operand, spec):
        operands.append(operand)
        specs.append(spec)

    add(filter_taps, pl.BlockSpec(filter_taps.shape, lambda b: (0, 0)))
    if half == 1:
        add(voltages, pl.BlockSpec((BLOCK, 8, nfft), lambda b: (b + low, frames // 8 - 1, 0)))
    else:
        add(before, pl.BlockSpec((BLOCK * past, nfft), lambda b: (b + low, 0)))
    for tile in range(tiles):
        add(voltages, pl.BlockSpec((BLOCK, frames, LANES), lambda b, t=tile: (b + low, half or 0, t)))
    scratch = []
    flops = 0
    for residue, fold in zip(residues, folds):
        depth = fold_terms(nfft, fold)
        for table in transform_table(nfft, ch_dev, count, step, residue):
            table = table.reshape(-1, depth)
            add(
                jnp.asarray(table),
                pl.BlockSpec(table.shape, lambda b: (0, 0), pipeline_mode=pl.Buffered(1)),
            )
        scratch += [pltpu.VMEM((BLOCK * frames, depth), jnp.bfloat16)] * 2
        flops += 6 * 2 * GROUP * count * depth * blocks * BLOCK * frames
    scratch.append(pltpu.VMEM((4, 8 + PAIR, LANES), jnp.float32))
    aliases = {}
    if has_base:
        aliases[len(operands)] = 0
        add(base, pl.BlockSpec(memory_space=pl.ANY))
    share = ROWS // len(places)
    return pl.pallas_call(
        functools.partial(transform_kernel, folds, tiles, has_base, len(places)),
        grid=(blocks,),
        out_shape=[jax.ShapeDtypeStruct((count, place[0] * share, LANES), jnp.float32) for place in places],
        input_output_aliases=aliases,
        in_specs=specs,
        out_specs=[
            pl.BlockSpec((count, share, LANES), lambda b, at=place[1]: (0, b + at, 0)) for place in places
        ],
        scratch_shapes=scratch,
        compiler_params=pltpu.CompilerParams(vmem_limit_bytes=VMEM_BYTES if half is None else 24 * 1024 * 1024),
        cost_estimate=pl.CostEstimate(
            flops=flops, bytes_accessed=4 * blocks * BLOCK * frames * nfft, transcendentals=0
        ),
        name="spectra_" + "_".join(map(str, residues)) + ("" if half is None else f"_half{half}"),
    )(*operands)


def correlate_kernel(n_inp, n_tm, frames, pieces, together, has_base, *rest):
    streams = []
    for number in pieces:
        streams.append(rest[:number])
        rest = rest[number:]
    (out,) = rest[has_base:]
    scale = 1.0 / (n_tm * frames)
    width = LANES // 2 // len(pieces)
    first = lax.broadcasted_iota(jnp.int32, (1, LANES), 1) % (2 * width) < width
    low_half = lax.broadcasted_iota(jnp.int32, (1, LANES), 1) < LANES // 2

    def payload(stream, sender, c):
        rows = slice(c * BLOCK, (c + 1) * BLOCK)
        return [
            array[sender, b, rows, :] for array in streams[stream] for b in range(array.shape[1])
        ]

    for c in range(together):
        columns = []
        for t in range(n_tm):
            senders = [p * n_tm + t for p in range(n_inp)]
            value = jnp.concatenate([x for s in senders for x in payload(0, s, c)], axis=0)
            if len(pieces) == 1:
                turned = pltpu.roll(value, width, 1)
                turned = jnp.where(first, turned, -turned)
            else:
                other = jnp.concatenate([x for s in senders for x in payload(1, s, c)], axis=0)
                turn = pl.program_id(1) * (LANES // 2)
                value = jnp.where(
                    low_half, pltpu.roll(value, turn, 1), pltpu.roll(other, LANES // 2 - turn, 1)
                )
                turned = jnp.where(
                    first, pltpu.roll(value, LANES - width, 1), -pltpu.roll(value, width, 1)
                )
            columns.append(split(value) + split(turned))
        p_hi, p_lo, t_hi, t_lo = [jnp.concatenate(column, axis=1) for column in zip(*columns)]
        right = jnp.concatenate([p_hi, p_hi, p_lo], axis=1)
        out[0, c, 0] = dot_nt(jnp.concatenate([p_hi, p_lo, p_hi], axis=1), right) * scale
        out[1, c, 0] = dot_nt(jnp.concatenate([t_hi, t_lo, t_hi], axis=1), right) * scale


def correlate(streams, base, n_inp, n_tm, inputs_dev, frames, ch_dev, step, residues, channels):
    count = n_inp * n_tm
    n_inputs = n_inp * inputs_dev
    has_base = int(base is not None)
    together = 2
    operands = []
    specs = []
    for stream in streams:
        for array, number, at in stream:
            operands.append(array.reshape(count, -1, (channels[1] - channels[0]) * BLOCK, LANES))
            specs.append(
                pl.BlockSpec(
                    (count, number, together * BLOCK, LANES),
                    lambda c, r, q=at // number: (0, q, c, 0),
                )
            )
    aliases = {}
    if has_base:
        aliases[len(operands)] = 0
        operands.append(base)
        specs.append(pl.BlockSpec(memory_space=pl.ANY))
    gap = residues[-1] - residues[0]
    pieces = [len(stream) for stream in streams]
    size = (channels[1] - channels[0]) * len(residues)
    skip = channels[0] // together
    return pl.pallas_call(
        functools.partial(correlate_kernel, n_inp, n_tm, frames, pieces, together, has_base),
        grid=((channels[1] - channels[0]) // together, len(residues)),
        out_shape=jax.ShapeDtypeStruct((2, GROUP, step, n_inputs, n_inputs), jnp.float32),
        in_specs=specs,
        out_specs=pl.BlockSpec(
            (2, together, 1, n_inputs, n_inputs), lambda c, r: (0, c + skip, residues[0] + gap * r, 0, 0)
        ),
        input_output_aliases=aliases,
        compiler_params=pltpu.CompilerParams(vmem_limit_bytes=62 * 1024 * 1024),
        cost_estimate=pl.CostEstimate(
            flops=12 * size * n_inputs * n_inputs * n_tm * LANES,
            bytes_accessed=4 * size * (n_inputs * n_tm * LANES + 2 * n_inputs * n_inputs),
            transcendentals=0,
        ),
        name="correlate_" + "_".join(map(str, residues)) + f"_from{channels[0]}",
    )(*operands)


def on_device(voltages, filter_taps):
    inputs_dev, frames, nfft = voltages.shape
    n_inp = lax.axis_size("inp")
    n_tm = lax.axis_size("tm")
    count = n_inp * n_tm
    ch_dev = nfft // 2 // count
    step = ch_dev // GROUP
    blocks = inputs_dev // BLOCK

    def history(tail):
        return lax.ppermute(tail, "tm", [(t, t + 1) for t in range(n_tm - 1)])

    def exchange(payload):
        return lax.all_to_all(payload, AXES, split_axis=0, concat_axis=0, tiled=True)

    def spectra(before, residues, half, *places):
        return transform(voltages, before, filter_taps, count, ch_dev, step, residues, half, *places)

    def visibilities(streams, base, residues, channels=(0, GROUP)):
        return correlate(
            streams, base, n_inp, n_tm, inputs_dev, frames, ch_dev, step, residues, channels
        )

    everything = (0, blocks)
    if step != 4 or blocks % 4:
        past = filter_taps.shape[0] - 1
        before = history(voltages[:, frames - past :, :].reshape(-1, nfft))
        result = None
        for residue in range(step):
            (sent,) = spectra(before, [residue], None, everything, (blocks, 0))
            result = visibilities([[(exchange(sent), blocks, 0)]], result, [residue])
        return result.reshape(2, ch_dev, *result.shape[3:])

    (first,) = spectra(None, [0, 2], 1, everything, (blocks, 0))
    got_first = exchange(first)
    before = history(last_frames(voltages, filter_taps.shape[0] - 1, first))
    size = 2 * blocks + blocks // 2
    (second,) = spectra(before, [0, 2], 0, everything, (size, 0))
    (second,) = spectra(before, [1], None, everything, (size, blocks, second))
    second, third = spectra(before, [3], None, everything, (2 * size, 4 * blocks, second), (blocks, 0))
    got_second = exchange(second)
    got_third = exchange(third)
    streams = [[(got_first, blocks, 0)], [(got_second, blocks, 0)]]
    result = visibilities(streams, None, [0, 2])
    result = visibilities([[(got_second, blocks, blocks)]], result, [1])
    result = visibilities([[(got_second, blocks, 4 * blocks)]], result, [3], (0, GROUP // 2))
    result = visibilities([[(got_third, blocks, 0)]], result, [3], (GROUP // 2, GROUP))
    return result.reshape(2, ch_dev, *result.shape[3:])


def solution(mesh):
    return jax.shard_map(
        on_device,
        mesh=mesh,
        in_specs=(P("inp", "tm", None), P()),
        out_specs=P(None, AXES, None, None),
        check_vma=False,
    )
```
